32 devices in a mesh: grp: 4 (over x, core), blk: 8 (over z, y).
Axes of the slice: x: 2, y: 2, z: 4, core: 2. Of those that a mesh axis runs over, the one named last changes fastest.
Arguments:
- integrals: bfloat16 [8192, 32768], P('blk', 'grp'), may hold values from -0.046875 to 0.046875
- block_mask: int32 [64, 256], P('blk', 'grp'), may hold values from 0 to 1, as said below
- amplitudes: bfloat16 [32768, 1024], P(('grp', 'blk')), may hold values from -6 to 6
- pair_batches: int32 [8], replicated, may hold values from 0 to 7, each once
Outputs:
- ladder: bfloat16 [1024, 8192], P('grp', 'blk')
The draws below stay inside these ranges and needn't reach their ends.
Inputs may be any that keep to these rules, and one draw needn't show every extreme that they name: `block_mask`: 0 or 1; the share of kept tiles rises from about a quarter in the first tile row to about three quarters in the last. `pair_batches`: each batch number once.
All inputs are finite; a program needn't handle non-finite values.
Results may differ from the reference program's by a relative error of at most 0.001.
Values may be sent and summed in bfloat16 or wider, within the bound.
A program may use at most 128 MiB of HBM per device.

```python
import jax
import jax.numpy as jnp
from jax import lax

BLOCK = 128
CD = 32768
BATCH = 128
NB = 8
AB_DEV = 1024
AB = 8192


def draw_block_mask(key, part):
    tile_rows = AB // BLOCK
    tile_cols = CD // BLOCK
    scores = jax.random.randint(jax.random.fold_in(key, 17), (tile_rows, tile_cols), 0, 1000)
    row_index = jnp.arange(tile_rows, dtype=jnp.int32)[:, None]
    limits = 250 + 500 * row_index // max(tile_rows - 1, 1)
    return (scores < limits).astype(jnp.int32)


def shard_levels(key, extent, shards, least, high):
    level, own = 1.0, jax.random.fold_in(key, 6)
    for axis_at, blocks in shards:
        steps = jnp.exp(jax.random.uniform(jax.random.fold_in(own, axis_at), (blocks,), jnp.float32, least / len(shards), high / len(shards)))
        level = level * jnp.repeat(steps, extent[axis_at] // blocks).reshape([-1 if axis == axis_at else 1 for axis in range(len(extent))])
    return level


def centred(own_key, dims, deviation, reach, split=(), held_as=jnp.bfloat16):
    drawn = jax.random.normal(own_key, dims, jnp.float32) * deviation
    if len(split) > 0:
        drawn = shard_levels(own_key, dims, split, -0.22, 0.18) * drawn
    return jnp.clip(drawn, min=-reach, max=reach).astype(held_as)


def setup_inputs(seed: int = 0) -> dict:
    streams_of = jax.random.split(jax.random.key(seed), 5)
    integrals = centred(streams_of[0], (AB, CD), (CD // 2) ** -0.5, 0.046875, ((0, 8), (1, 4)))
    block_mask = draw_block_mask(jax.random.fold_in(streams_of[4], 71), 0)
    amplitudes = centred(streams_of[2], (CD, NB * BATCH), 1.0, 6.0, ((0, 32),))
    pair_batches = jax.random.permutation(streams_of[3], NB).astype(jnp.int32)
    return dict(integrals=integrals, block_mask=block_mask, amplitudes=amplitudes, pair_batches=pair_batches)


def reference(integrals, block_mask, amplitudes, pair_batches):
    rows_in = amplitudes.shape[0]
    grouped = amplitudes.reshape(rows_in, NB, BATCH)
    chosen = jnp.take(grouped, pair_batches.astype(jnp.int32), axis=1).reshape(rows_in, NB * BATCH)
    rows_total = integrals.shape[0]
    widths = integrals.shape[1]
    steps_total = rows_total // AB_DEV

    def one_slab(position):
        vrows = lax.dynamic_slice_in_dim(integrals, position * AB_DEV, AB_DEV, 0)
        mrows = lax.dynamic_slice_in_dim(block_mask, position * (AB_DEV // BLOCK), AB_DEV // BLOCK, 0)
        weights = mrows.astype(integrals.dtype)[:, None, :, None]
        masked = (vrows.reshape(AB_DEV // BLOCK, BLOCK, widths // BLOCK, BLOCK) * weights).reshape(AB_DEV, widths)
        return lax.dot_general(chosen, masked, (((0,), (1,)), ((), ())), preferred_element_type=jnp.float32)

    slabs = lax.map(one_slab, jnp.arange(steps_total, dtype=jnp.int32))
    result = jnp.transpose(slabs, (1, 0, 2)).reshape(NB * BATCH, rows_total)
    return result.astype(jnp.bfloat16)
```

```python
import functools

import jax
import jax.numpy as jnp
from jax import lax
from jax.experimental import pallas as pl
from jax.experimental.pallas import tpu as pltpu
from jax.sharding import PartitionSpec as P

BLOCK = 128
BATCH = 128
NB = 8
LAG = 2
MESH = pl.DeviceIdType.MESH


def plain(integrals, block_mask, amplitudes, pair_batches):
    rows_in = amplitudes.shape[0]
    grouped = amplitudes.reshape(rows_in, NB, BATCH)
    chosen = jnp.take(grouped, pair_batches, axis=1).reshape(rows_in, NB * BATCH)
    out_rows = integrals.shape[0]
    fragment = lax.all_gather(chosen, "blk", axis=0, tiled=True)
    number = fragment.shape[0]
    mcols = block_mask.astype(jnp.bfloat16)
    tiled = (
        integrals.reshape(out_rows // BLOCK, BLOCK, number // BLOCK, BLOCK)
        * mcols[:, None, :, None]
    )
    masked = tiled.reshape(out_rows, number)
    partial_sum = lax.dot_general(
        fragment, masked, (((0,), (1,)), ((), ())), preferred_element_type=jnp.float32
    )
    owned = lax.psum_scatter(partial_sum, "grp", scatter_dimension=0, tiled=True)
    return owned.astype(jnp.bfloat16)


def kernel(
    nz, beta,
    mask_ref, amp_ref, int_ref, out_ref,
    T, V, acc, sib, far,
    v_sem, zfs, zbs, zfr, zbr, yas, yar, ybs, ybr, sibs, sibr, fars, farr,
):
    g, b = lax.axis_index("grp"), lax.axis_index("blk")
    x, c = g // 2, g % 2
    z, y = b // 2, b % 2
    Q, nb, R, _ = T.shape
    pairs = Q // 2
    rows_out = V.shape[0]
    alpha = R - beta
    has_l, has_r = z > 0, z < nz - 1
    sibling = (x * 2 + 1 - c, b)
    opposite = ((1 - x) * 2 + c, b)
    partner = (g, z * 2 + 1 - y)
    toward = ((g, jnp.minimum(z + 1, nz - 1) * 2 + y), (g, jnp.maximum(z - 1, 0) * 2 + y))

    def remote(src, dst, send, recv, device):
        return pltpu.make_async_remote_copy(
            src_ref=src, dst_ref=dst, send_sem=send, recv_sem=recv,
            device_id=device, device_id_type=MESH,
        )

    def z_full(q, o, d):
        ref = T.at[q, 2 * o + y]
        return remote(ref, ref, zfs.at[q, d, o], zfr.at[q, o], toward[d])

    def z_part(q, o, d):
        ref = T.at[q, 2 * o + 1 - y, pl.ds(alpha, beta)]
        return remote(ref, ref, zbs.at[q, d, o], zbr.at[q, o], toward[d])

    def y_first(q, o, v):
        ref = T.at[q, 2 * o + v, pl.ds(0, alpha)]
        return remote(ref, ref, yas.at[q, o], yar.at[q, o], partner)

    def y_last(q, v):
        ref = T.at[q, 2 * z + v, pl.ds(alpha, beta)]
        return remote(ref, ref, ybs.at[q], ybr.at[q], partner)

    def to_sibling(q, j):
        return remote(acc.at[q], sib.at[j], sibs.at[j], sibr.at[j], sibling)

    def to_opposite(q, j):
        return remote(acc.at[q, 1 - x], far.at[j], fars.at[j], farr.at[j], opposite)

    load_v = pltpu.make_async_copy(int_ref, V, v_sem)
    load_v.start()

    barrier = pltpu.get_barrier_semaphore()
    for device in (sibling, opposite, partner):
        pl.semaphore_signal(barrier, inc=1, device_id=device, device_id_type=MESH)
    for d, there in ((0, has_r), (1, has_l)):
        @pl.when(there)
        def _():
            pl.semaphore_signal(barrier, inc=1, device_id=toward[d], device_id_type=MESH)

    def choose(q):
        for half in range(2):
            k = (NB // 2) * half + (NB // 4) * (q % 2) + q // 2
            T[q, b, :, half * BATCH:(half + 1) * BATCH] = amp_ref[:, k * BATCH:(k + 1) * BATCH]

    choose(0)
    choose(1)
    pl.semaphore_wait(barrier, 3 + has_r.astype(jnp.int32) + has_l.astype(jnp.int32))

    def gemm(q, shard):
        tile = min(256, rows_out)

        def rows_of(i, _):
            rows = pl.ds(pl.multiple_of(i * tile, tile), tile)
            cols = pl.ds(pl.multiple_of(shard * R, 128), R)
            res = jnp.dot(V[rows, cols], T[q, shard], preferred_element_type=jnp.float32)
            acc[q, 0, rows, :] += res[:, :BATCH]
            acc[q, 1, rows, :] += res[:, BATCH:]
            return 0

        lax.fori_loop(0, rows_out // tile, rows_of, 0)

    def start_own(p):
        for qi in range(2):
            q = 2 * p + qi
            y_last(q, y).start()
            for d, there in ((0, has_r), (1, has_l)):
                @pl.when(there)
                def _():
                    z_full(q, z, d).start()
            y_first(q, z, y).start()
        for qi in range(2):
            q = 2 * p + qi
            y_last(q, 1 - y).wait_recv()
            for d, there in ((0, has_r), (1, has_l)):
                @pl.when(there)
                def _():
                    z_part(q, z, d).start()

    def forward(p, s):
        for qi in range(2):
            q = 2 * p + qi
            for d, there in ((0, has_r), (1, has_l)):
                o = z - s if d == 0 else z + s

                @pl.when((o >= 0) & (o < nz))
                def _():
                    z_full(q, o, d).wait_recv()

                    @pl.when(there)
                    def _():
                        z_full(q, o, d).start()

                    y_first(q, o, y).start()
                    z_part(q, o, d).wait_recv()

                    @pl.when(there)
                    def _():
                        z_part(q, o, d).start()

    def each(p, s, act):
        def one(i, _):
            q, d = 2 * p + i // 2, i % 2
            o = z + s * (2 * d - 1)

            @pl.when((o >= 0) & (o < nz) & ((d == 0) | (s > 0)))
            def _():
                act(q, o)
            return 0

        lax.fori_loop(0, 4, one, 0)

    def lagged(q, o):
        y_first(q, o, 1 - y).wait_recv()
        gemm(q, 2 * o + 1 - y)

    def reduce_a(p):
        for qi in range(2):
            @pl.when(c != qi)
            def _():
                to_sibling(2 * p + qi, p).start()

    def reduce_b(p):
        q = 2 * p + c
        to_sibling(q, p).wait_recv()
        acc[q, 1 - x] += sib[p, 1 - x]
        to_opposite(q, p).start()
        acc[q, x] += sib[p, x]

    def reduce_c(p):
        q = 2 * p + c
        to_opposite(q, p).wait_recv()

        def cols(i, _):
            rows = pl.ds(pl.multiple_of(i * BLOCK, BLOCK), BLOCK)
            total = acc[q, x, rows, :] + far[p, rows, :]
            out_ref[pl.ds(pl.multiple_of(p * BATCH, BATCH), BATCH), rows] = total.T.astype(jnp.bfloat16)
            return 0

        lax.fori_loop(0, rows_out // BLOCK, cols, 0)

    def mask_tiles():
        def tile(i, _):
            r, k = i // (V.shape[1] // BLOCK), i % (V.shape[1] // BLOCK)
            at = (
                pl.ds(pl.multiple_of(r * BLOCK, BLOCK), BLOCK),
                pl.ds(pl.multiple_of(k * BLOCK, BLOCK), BLOCK),
            )
            keep = jnp.full((BLOCK, BLOCK), mask_ref[r, k].astype(jnp.float32)).astype(jnp.bfloat16)
            V[at] = V[at] * keep
            return 0

        lax.fori_loop(0, (rows_out // BLOCK) * (V.shape[1] // BLOCK), tile, 0)

    def step(t, _):
        p, s = t // nz, t % nz

        @pl.when(t < pairs * nz)
        def _():
            @pl.when(s == 0)
            def _():
                start_own(p)

            @pl.when(s > 0)
            def _():
                forward(p, s)

            @pl.when(t == 0)
            def _():
                for q in range(2, Q):
                    choose(q)
                acc[...] = jnp.zeros_like(acc)
                load_v.wait()
                mask_tiles()

            each(p, s, lambda q, o: gemm(q, 2 * o + y))

        @pl.when(t >= LAG)
        def _():
            late = jnp.maximum(t - LAG, 0)
            each(late // nz, late % nz, lagged)

        done = p - 1
        for at, act in ((LAG - 1, reduce_a), (LAG, reduce_b), (LAG + 1, reduce_c)):
            @pl.when((done >= 0) & (done < pairs - 1) & (s == at))
            def _():
                act(done)
        return 0

    lax.fori_loop(0, pairs * nz + LAG, step, 0)
    for act in (reduce_a, reduce_b, reduce_c):
        act(pairs - 1)

    def drain(i, _):
        q, o = i // nz, i % nz

        @pl.when((o <= z) & has_r)
        def _():
            z_full(q, o, 0).wait_send()
            z_part(q, o, 0).wait_send()

        @pl.when((o >= z) & has_l)
        def _():
            z_full(q, o, 1).wait_send()
            z_part(q, o, 1).wait_send()

        y_first(q, o, y).wait_send()
        return 0

    lax.fori_loop(0, Q * nz, drain, 0)
    for q in range(Q):
        y_last(q, y).wait_send()
    for p in range(pairs):
        to_sibling(2 * p + 1 - c, p).wait_send()
        to_opposite(2 * p + c, p).wait_send()


def fused(nb, integrals, block_mask, amplitudes, pair_batches):
    rows_out, number = integrals.shape
    R, occ = amplitudes.shape
    Q, nz = NB // 2, nb // 2
    beta = max(16, R // 6 // 16 * 16)
    chosen = jnp.take(amplitudes.reshape(R, NB, BATCH), pair_batches, axis=1).reshape(R, occ)
    dma = pltpu.SemaphoreType.DMA
    return pl.pallas_call(
        functools.partial(kernel, nz, beta),
        out_shape=jax.ShapeDtypeStruct((occ // 4, rows_out), jnp.bfloat16),
        in_specs=[
            pl.BlockSpec(memory_space=pltpu.SMEM),
            pl.BlockSpec(memory_space=pltpu.VMEM),
            pl.BlockSpec(memory_space=pl.ANY),
        ],
        out_specs=pl.BlockSpec(memory_space=pltpu.VMEM),
        scratch_shapes=[
            pltpu.VMEM((Q, nb, R, 2 * BATCH), jnp.bfloat16),
            pltpu.VMEM((rows_out, number), jnp.bfloat16),
            pltpu.VMEM((Q, 2, rows_out, BATCH), jnp.float32),
            pltpu.VMEM((Q // 2, 2, rows_out, BATCH), jnp.float32),
            pltpu.VMEM((Q // 2, rows_out, BATCH), jnp.float32),
            dma,
            dma((Q, 2, nz)), dma((Q, 2, nz)), dma((Q, nz)), dma((Q, nz)),
            dma((Q, nz)), dma((Q, nz)), dma((Q,)), dma((Q,)),
            dma((Q // 2,)), dma((Q // 2,)), dma((Q // 2,)), dma((Q // 2,)),
        ],
        compiler_params=pltpu.CompilerParams(
            collective_id=0, has_side_effects=True, vmem_limit_bytes=56 * 2**20
        ),
        cost_estimate=pl.CostEstimate(
            flops=2 * occ * rows_out * number,
            bytes_accessed=2 * rows_out * number + 2 * nb * R * occ,
            transcendentals=0,
        ),
    )(block_mask, chosen, integrals)


def solution(mesh):
    ng, nb = mesh.shape["grp"], mesh.shape["blk"]
    takes = ng == 4 and nb % 2 == 0 and nb // 2 >= LAG + 2
    in_specs = (P("blk", "grp"), P("blk", "grp"), P(("grp", "blk"), None), P())
    return jax.shard_map(
        functools.partial(fused, nb) if takes else plain,
        mesh=mesh, in_specs=in_specs, out_specs=P("grp", "blk"), check_vma=False,
    )
```

```python
import functools

import jax
import jax.numpy as jnp
from jax import lax
from jax.experimental import pallas as pl
from jax.experimental.pallas import tpu as pltpu
from jax.sharding import PartitionSpec as P

BLOCK = 128
BATCH = 128
NB = 8
LAG = 2
MESH = pl.DeviceIdType.MESH


def plain(integrals, block_mask, amplitudes, pair_batches):
    rows_in = amplitudes.shape[0]
    grouped = amplitudes.reshape(rows_in, NB, BATCH)
    chosen = jnp.take(grouped, pair_batches, axis=1).reshape(rows_in, NB * BATCH)
    out_rows = integrals.shape[0]
    fragment = lax.all_gather(chosen, "blk", axis=0, tiled=True)
    number = fragment.shape[0]
    mcols = block_mask.astype(jnp.bfloat16)
    tiled = (
        integrals.reshape(out_rows // BLOCK, BLOCK, number // BLOCK, BLOCK)
        * mcols[:, None, :, None]
    )
    masked = tiled.reshape(out_rows, number)
    partial_sum = lax.dot_general(
        fragment, masked, (((0,), (1,)), ((), ())), preferred_element_type=jnp.float32
    )
    owned = lax.psum_scatter(partial_sum, "grp", scatter_dimension=0, tiled=True)
    return owned.astype(jnp.bfloat16)


def kernel(
    nz, beta,
    mask_ref, order_ref, amp_ref, int_ref, out_ref,
    T, V, acc, sib, far,
    v_sem, zfs, zbs, zfr, zbr, yas, yar, ybs, ybr, sibs, sibr, fars, farr,
):
    g, b = lax.axis_index("grp"), lax.axis_index("blk")
    x, c = g // 2, g % 2
    z, y = b // 2, b % 2
    Q, nb, R, _ = T.shape
    pairs = Q // 2
    rows_out = V.shape[0]
    alpha = R - beta
    has_l, has_r = z > 0, z < nz - 1
    sibling = (x * 2 + 1 - c, b)
    opposite = ((1 - x) * 2 + c, b)
    partner = (g, z * 2 + 1 - y)
    toward = ((g, jnp.minimum(z + 1, nz - 1) * 2 + y), (g, jnp.maximum(z - 1, 0) * 2 + y))

    def remote(src, dst, send, recv, device):
        return pltpu.make_async_remote_copy(
            src_ref=src, dst_ref=dst, send_sem=send, recv_sem=recv,
            device_id=device, device_id_type=MESH,
        )

    def z_full(q, o, d):
        ref = T.at[q, 2 * o + y]
        return remote(ref, ref, zfs.at[q, d, o], zfr.at[q, o], toward[d])

    def z_part(q, o, d):
        ref = T.at[q, 2 * o + 1 - y, pl.ds(alpha, beta)]
        return remote(ref, ref, zbs.at[q, d, o], zbr.at[q, o], toward[d])

    def y_first(q, o, v):
        ref = T.at[q, 2 * o + v, pl.ds(0, alpha)]
        return remote(ref, ref, yas.at[q, o], yar.at[q, o], partner)

    def y_last(q, v):
        ref = T.at[q, 2 * z + v, pl.ds(alpha, beta)]
        return remote(ref, ref, ybs.at[q], ybr.at[q], partner)

    def to_sibling(q, j, h):
        return remote(acc.at[q, h], sib.at[j, h], sibs.at[j, h], sibr.at[j, h], sibling)

    def to_opposite(q, j):
        return remote(acc.at[q, 1 - x], far.at[j], fars.at[j], farr.at[j], opposite)

    load_v = pltpu.make_async_copy(int_ref, V, v_sem)
    load_v.start()

    barrier = pltpu.get_barrier_semaphore()
    for device in (sibling, opposite, partner):
        pl.semaphore_signal(barrier, inc=1, device_id=device, device_id_type=MESH)
    for d, there in ((0, has_r), (1, has_l)):
        @pl.when(there)
        def _():
            pl.semaphore_signal(barrier, inc=1, device_id=toward[d], device_id_type=MESH)

    def choose(q):
        for half in range(2):
            k = (NB // 2) * half + (NB // 4) * (q % 2) + q // 2
            picks = [
                jnp.full((16, BATCH), jnp.where(order_ref[k] == n, 1.0, 0.0)).astype(jnp.bfloat16)
                for n in range(NB)
            ]

            def some(i, _):
                rows = pl.ds(pl.multiple_of(i * 128, 128), 128)
                total = None
                for n in range(NB):
                    batch = amp_ref[rows, n * BATCH:(n + 1) * BATCH]
                    term = batch * jnp.tile(picks[n], (8, 1))
                    total = term if total is None else total + term
                T[q, b, rows, half * BATCH:(half + 1) * BATCH] = total
                return 0

            lax.fori_loop(0, R // 128, some, 0)

    choose(0)
    choose(1)
    pl.semaphore_wait(barrier, 3 + has_r.astype(jnp.int32) + has_l.astype(jnp.int32))

    def gemm(q, shard):
        tile = min(256, rows_out)

        @pl.when(q == 0)
        def _():
            mask_tiles(shard)

        def rows_of(i, _):
            rows = pl.ds(pl.multiple_of(i * tile, tile), tile)
            cols = pl.ds(pl.multiple_of(shard * R, 128), R)
            res = jnp.dot(V[rows, cols], T[q, shard], preferred_element_type=jnp.float32)
            acc[q, 0, rows, :] += res[:, :BATCH]
            acc[q, 1, rows, :] += res[:, BATCH:]
            return 0

        lax.fori_loop(0, rows_out // tile, rows_of, 0)

    def start_own(p):
        for qi in range(2):
            q = 2 * p + qi
            y_last(q, y).start()
            for d, there in ((0, has_r), (1, has_l)):
                @pl.when(there)
                def _():
                    z_full(q, z, d).start()
            y_first(q, z, y).start()
        for qi in range(2):
            q = 2 * p + qi
            y_last(q, 1 - y).wait_recv()
            for d, there in ((0, has_r), (1, has_l)):
                @pl.when(there)
                def _():
                    z_part(q, z, d).start()

    def forward(p, s):
        for qi in range(2):
            q = 2 * p + qi
            for d, there in ((0, has_r), (1, has_l)):
                o = z - s if d == 0 else z + s

                @pl.when((o >= 0) & (o < nz))
                def _():
                    z_full(q, o, d).wait_recv()

                    @pl.when(there)
                    def _():
                        z_full(q, o, d).start()

                    y_first(q, o, y).start()
                    z_part(q, o, d).wait_recv()

                    @pl.when(there)
                    def _():
                        z_part(q, o, d).start()

    def each(p, s, act):
        def one(i, _):
            q, d = 2 * p + i // 2, i % 2
            o = z + s * (2 * d - 1)

            @pl.when((o >= 0) & (o < nz) & ((d == 0) | (s > 0)))
            def _():
                act(q, o)
            return 0

        lax.fori_loop(0, 4, one, 0)

    def lagged(q, o):
        y_first(q, o, 1 - y).wait_recv()
        gemm(q, 2 * o + 1 - y)

    def reduce_a(p):
        for qi in range(2):
            @pl.when(c != qi)
            def _():
                to_sibling(2 * p + qi, p, 1 - x).start()
                to_sibling(2 * p + qi, p, x).start()

    def reduce_b(p):
        q = 2 * p + c
        to_sibling(q, p, 1 - x).wait_recv()
        acc[q, 1 - x] += sib[p, 1 - x]
        to_opposite(q, p).start()
        to_sibling(q, p, x).wait_recv()
        acc[q, x] += sib[p, x]

    def reduce_c(p):
        q = 2 * p + c
        to_opposite(q, p).wait_recv()

        def cols(i, _):
            rows = pl.ds(pl.multiple_of(i * BLOCK, BLOCK), BLOCK)
            total = acc[q, x, rows, :] + far[p, rows, :]
            out_ref[pl.ds(pl.multiple_of(p * BATCH, BATCH), BATCH), rows] = total.T.astype(jnp.bfloat16)
            return 0

        lax.fori_loop(0, rows_out // BLOCK, cols, 0)

    def mask_tiles(shard):
        def tile(i, _):
            r, k = i // (R // BLOCK), shard * (R // BLOCK) + i % (R // BLOCK)
            at = (
                pl.ds(pl.multiple_of(r * BLOCK, BLOCK), BLOCK),
                pl.ds(pl.multiple_of(k * BLOCK, BLOCK), BLOCK),
            )
            keep = jnp.full((BLOCK, BLOCK), mask_ref[r, k].astype(jnp.float32)).astype(jnp.bfloat16)
            V[at] = V[at] * keep
            return 0

        lax.fori_loop(0, (rows_out // BLOCK) * (R // BLOCK), tile, 0)

    def step(t, _):
        p, s = t // nz, t % nz

        @pl.when(t < pairs * nz)
        def _():
            @pl.when(s == 0)
            def _():
                start_own(p)

            @pl.when(s > 0)
            def _():
                forward(p, s)

            @pl.when(t == 0)
            def _():
                for q in range(2, Q):
                    choose(q)
                acc[...] = jnp.zeros_like(acc)
                load_v.wait()

            each(p, s, lambda q, o: gemm(q, 2 * o + y))

        @pl.when(t >= LAG)
        def _():
            late = jnp.maximum(t - LAG, 0)
            each(late // nz, late % nz, lagged)

        done = p - 1
        for at, act in ((LAG - 1, reduce_a), (LAG, reduce_b), (LAG + 1, reduce_c)):
            @pl.when((done >= 0) & (done < pairs - 1) & (s == at))
            def _():
                act(done)
        return 0

    lax.fori_loop(0, pairs * nz + LAG, step, 0)
    for act in (reduce_a, reduce_b, reduce_c):
        act(pairs - 1)

    def drain(i, _):
        q, o = i // nz, i % nz

        @pl.when((o <= z) & has_r)
        def _():
            z_full(q, o, 0).wait_send()
            z_part(q, o, 0).wait_send()

        @pl.when((o >= z) & has_l)
        def _():
            z_full(q, o, 1).wait_send()
            z_part(q, o, 1).wait_send()

        y_first(q, o, y).wait_send()
        return 0

    lax.fori_loop(0, Q * nz, drain, 0)
    for q in range(Q):
        y_last(q, y).wait_send()
    for p in range(pairs):
        for h in range(2):
            to_sibling(2 * p + 1 - c, p, h).wait_send()
        to_opposite(2 * p + c, p).wait_send()


def fused(nb, integrals, block_mask, amplitudes, pair_batches):
    rows_out, number = integrals.shape
    R, occ = amplitudes.shape
    Q, nz = NB // 2, nb // 2
    beta = max(16, R // 6 // 16 * 16)
    dma = pltpu.SemaphoreType.DMA
    return pl.pallas_call(
        functools.partial(kernel, nz, beta),
        out_shape=jax.ShapeDtypeStruct((occ // 4, rows_out), jnp.bfloat16),
        in_specs=[
            pl.BlockSpec(memory_space=pltpu.SMEM),
            pl.BlockSpec(memory_space=pltpu.SMEM),
            pl.BlockSpec(memory_space=pltpu.VMEM),
            pl.BlockSpec(memory_space=pl.ANY),
        ],
        out_specs=pl.BlockSpec(memory_space=pltpu.VMEM),
        scratch_shapes=[
            pltpu.VMEM((Q, nb, R, 2 * BATCH), jnp.bfloat16),
            pltpu.VMEM((rows_out, number), jnp.bfloat16),
            pltpu.VMEM((Q, 2, rows_out, BATCH), jnp.float32),
            pltpu.VMEM((Q // 2, 2, rows_out, BATCH), jnp.float32),
            pltpu.VMEM((Q // 2, rows_out, BATCH), jnp.float32),
            dma,
            dma((Q, 2, nz)), dma((Q, 2, nz)), dma((Q, nz)), dma((Q, nz)),
            dma((Q, nz)), dma((Q, nz)), dma((Q,)), dma((Q,)),
            dma((Q // 2, 2)), dma((Q // 2, 2)), dma((Q // 2,)), dma((Q // 2,)),
        ],
        compiler_params=pltpu.CompilerParams(
            collective_id=0, has_side_effects=True, vmem_limit_bytes=56 * 2**20
        ),
        cost_estimate=pl.CostEstimate(
            flops=2 * occ * rows_out * number,
            bytes_accessed=2 * rows_out * number + 2 * nb * R * occ,
            transcendentals=0,
        ),
    )(block_mask, pair_batches, amplitudes, integrals)


def solution(mesh):
    ng, nb = mesh.shape["grp"], mesh.shape["blk"]
    takes = ng == 4 and nb % 2 == 0 and nb // 2 >= LAG + 2
    in_specs = (P("blk", "grp"), P("blk", "grp"), P(("grp", "blk"), None), P())
    return jax.shard_map(
        functools.partial(fused, nb) if takes else plain,
        mesh=mesh, in_specs=in_specs, out_specs=P("grp", "blk"), check_vma=False,
    )
```

```python
import functools

import jax
import jax.numpy as jnp
from jax import lax
from jax.experimental import pallas as pl
from jax.experimental.pallas import tpu as pltpu
from jax.sharding import PartitionSpec as P

BLOCK = 128
BATCH = 128
NB = 8
LAG = 2
MESH = pl.DeviceIdType.MESH


def plain(integrals, block_mask, amplitudes, pair_batches):
    rows_in = amplitudes.shape[0]
    grouped = amplitudes.reshape(rows_in, NB, BATCH)
    chosen = jnp.take(grouped, pair_batches, axis=1).reshape(rows_in, NB * BATCH)
    out_rows = integrals.shape[0]
    fragment = lax.all_gather(chosen, "blk", axis=0, tiled=True)
    number = fragment.shape[0]
    mcols = block_mask.astype(jnp.bfloat16)
    tiled = (
        integrals.reshape(out_rows // BLOCK, BLOCK, number // BLOCK, BLOCK)
        * mcols[:, None, :, None]
    )
    masked = tiled.reshape(out_rows, number)
    partial_sum = lax.dot_general(
        fragment, masked, (((0,), (1,)), ((), ())), preferred_element_type=jnp.float32
    )
    owned = lax.psum_scatter(partial_sum, "grp", scatter_dimension=0, tiled=True)
    return owned.astype(jnp.bfloat16)


def kernel(
    nz, beta,
    mask_ref, order_ref, amp_ref, int_ref, out_ref,
    T, V, acc, sib, far,
    v_sem, zfs, zbs, zfr, zbr, yas, yar, ybs, ybr, sibs, sibr, fars, farr,
):
    g, b = lax.axis_index("grp"), lax.axis_index("blk")
    x, c = g // 2, g % 2
    z, y = b // 2, b % 2
    Q, nb, R, _ = T.shape
    pairs = Q // 2
    rows_out = V.shape[0]
    alpha = R - beta
    has_l, has_r = z > 0, z < nz - 1
    sibling = (x * 2 + 1 - c, b)
    opposite = ((1 - x) * 2 + c, b)
    partner = (g, z * 2 + 1 - y)
    toward = ((g, jnp.minimum(z + 1, nz - 1) * 2 + y), (g, jnp.maximum(z - 1, 0) * 2 + y))

    def remote(src, dst, send, recv, device):
        return pltpu.make_async_remote_copy(
            src_ref=src, dst_ref=dst, send_sem=send, recv_sem=recv,
            device_id=device, device_id_type=MESH,
        )

    def z_full(q, o, d):
        ref = T.at[q, 2 * o + y]
        return remote(ref, ref, zfs.at[q, d, o], zfr.at[q, o], toward[d])

    def z_part(q, o, d):
        ref = T.at[q, 2 * o + 1 - y, pl.ds(alpha, beta)]
        return remote(ref, ref, zbs.at[q, d, o], zbr.at[q, o], toward[d])

    def y_first(q, o, v):
        ref = T.at[q, 2 * o + v, pl.ds(0, alpha)]
        return remote(ref, ref, yas.at[q, o], yar.at[q, o], partner)

    def y_last(q, v):
        ref = T.at[q, 2 * z + v, pl.ds(alpha, beta)]
        return remote(ref, ref, ybs.at[q], ybr.at[q], partner)

    def to_sibling(q, j, h):
        return remote(acc.at[q, h], sib.at[j, h], sibs.at[j, h], sibr.at[j, h], sibling)

    def to_opposite(q, j):
        return remote(acc.at[q, 1 - x], far.at[j], fars.at[j], farr.at[j], opposite)

    load_v = pltpu.make_async_copy(int_ref, V, v_sem)
    load_v.start()

    barrier = pltpu.get_barrier_semaphore()
    for device in (sibling, opposite, partner):
        pl.semaphore_signal(barrier, inc=1, device_id=device, device_id_type=MESH)
    for d, there in ((0, has_r), (1, has_l)):
        @pl.when(there)
        def _():
            pl.semaphore_signal(barrier, inc=1, device_id=toward[d], device_id_type=MESH)

    def choose(q):
        for half in range(2):
            k = (NB // 2) * half + (NB // 4) * (q % 2) + q // 2
            picks = [
                jnp.full((16, BATCH), jnp.where(order_ref[k] == n, 1.0, 0.0)).astype(jnp.bfloat16)
                for n in range(NB)
            ]

            def some(i, _):
                rows = pl.ds(pl.multiple_of(i * 128, 128), 128)
                total = None
                for n in range(NB):
                    batch = amp_ref[rows, n * BATCH:(n + 1) * BATCH]
                    term = batch * jnp.tile(picks[n], (8, 1))
                    total = term if total is None else total + term
                T[q, b, rows, half * BATCH:(half + 1) * BATCH] = total
                return 0

            lax.fori_loop(0, R // 128, some, 0)

    choose(0)
    choose(1)
    pl.semaphore_wait(barrier, 3 + has_r.astype(jnp.int32) + has_l.astype(jnp.int32))

    def gemm(q, shard):
        tile = min(256, rows_out)

        @pl.when(q == 0)
        def _():
            mask_tiles(shard)

        def rows_of(i, _):
            rows = pl.ds(pl.multiple_of(i * tile, tile), tile)
            cols = pl.ds(pl.multiple_of(shard * R, 128), R)
            res = jnp.dot(V[rows, cols], T[q, shard], preferred_element_type=jnp.float32)
            acc[q, 0, rows, :] += res[:, :BATCH]
            acc[q, 1, rows, :] += res[:, BATCH:]
            return 0

        lax.fori_loop(0, rows_out // tile, rows_of, 0)

    def start_own(p):
        for qi in range(2):
            q = 2 * p + qi
            y_last(q, y).start()
            for d, there in ((0, has_r), (1, has_l)):
                @pl.when(there)
                def _():
                    z_full(q, z, d).start()
            y_first(q, z, y).start()
        for qi in range(2):
            q = 2 * p + qi
            y_last(q, 1 - y).wait_recv()
            for d, there in ((0, has_r), (1, has_l)):
                @pl.when(there)
                def _():
                    z_part(q, z, d).start()

    def forward(p, s):
        for qi in range(2):
            q = 2 * p + qi
            for d, there in ((0, has_r), (1, has_l)):
                o = z - s if d == 0 else z + s

                @pl.when((o >= 0) & (o < nz))
                def _():
                    z_full(q, o, d).wait_recv()

                    @pl.when(there)
                    def _():
                        z_full(q, o, d).start()

                    y_first(q, o, y).start()
                    z_part(q, o, d).wait_recv()

                    @pl.when(there)
                    def _():
                        z_part(q, o, d).start()

    def each(p, s, act, low=0, high=4):
        def one(i, _):
            q, d = 2 * p + i // 2, i % 2
            o = z + s * (2 * d - 1)

            @pl.when((o >= 0) & (o < nz) & ((d == 0) | (s > 0)))
            def _():
                act(q, o)
            return 0

        lax.fori_loop(low, high, one, 0)

    def lagged(q, o):
        y_first(q, o, 1 - y).wait_recv()
        gemm(q, 2 * o + 1 - y)

    def hand_over(p, qi):
        @pl.when(c != qi)
        def _():
            to_sibling(2 * p + qi, p, 1 - x).start()
            to_sibling(2 * p + qi, p, x).start()

    def reduce_a(p):
        for qi in range(2):
            hand_over(p, qi)

    def reduce_b(p):
        q = 2 * p + c
        to_sibling(q, p, 1 - x).wait_recv()
        acc[q, 1 - x] += sib[p, 1 - x]
        to_opposite(q, p).start()
        to_sibling(q, p, x).wait_recv()
        acc[q, x] += sib[p, x]

    def reduce_c(p):
        q = 2 * p + c
        to_opposite(q, p).wait_recv()

        def cols(i, _):
            rows = pl.ds(pl.multiple_of(i * BLOCK, BLOCK), BLOCK)
            total = acc[q, x, rows, :] + far[p, rows, :]
            out_ref[pl.ds(pl.multiple_of(p * BATCH, BATCH), BATCH), rows] = total.T.astype(jnp.bfloat16)
            return 0

        lax.fori_loop(0, rows_out // BLOCK, cols, 0)

    def mask_tiles(shard):
        def tile(i, _):
            r, k = i // (R // BLOCK), shard * (R // BLOCK) + i % (R // BLOCK)
            at = (
                pl.ds(pl.multiple_of(r * BLOCK, BLOCK), BLOCK),
                pl.ds(pl.multiple_of(k * BLOCK, BLOCK), BLOCK),
            )
            keep = jnp.full((BLOCK, BLOCK), mask_ref[r, k].astype(jnp.float32)).astype(jnp.bfloat16)
            V[at] = V[at] * keep
            return 0

        lax.fori_loop(0, (rows_out // BLOCK) * (R // BLOCK), tile, 0)

    def step(t, _):
        p, s = t // nz, t % nz

        @pl.when(t < pairs * nz)
        def _():
            @pl.when(s == 0)
            def _():
                start_own(p)

            @pl.when(s > 0)
            def _():
                forward(p, s)

            @pl.when(t == 0)
            def _():
                for q in range(2, Q):
                    choose(q)
                acc[...] = jnp.zeros_like(acc)
                load_v.wait()

            each(p, s, lambda q, o: gemm(q, 2 * o + y))

        @pl.when(t >= LAG)
        def _():
            late = jnp.maximum(t - LAG, 0)
            each(late // nz, late % nz, lagged)

        done = p - 1
        for at, act in ((LAG - 1, reduce_a), (LAG, reduce_b), (LAG + 1, reduce_c)):
            @pl.when((done >= 0) & (done < pairs - 1) & (s == at))
            def _():
                act(done)
        return 0

    lax.fori_loop(0, pairs * nz + LAG - 1, step, 0)
    last = pairs - 1
    for qi in range(2):
        each(last, nz - 1, lagged, 2 * qi, 2 * qi + 2)
        hand_over(last, qi)

        @pl.when(c == qi)
        def _():
            reduce_b(last)

    reduce_c(last)

    def drain(i, _):
        q, o = i // nz, i % nz

        @pl.when((o <= z) & has_r)
        def _():
            z_full(q, o, 0).wait_send()
            z_part(q, o, 0).wait_send()

        @pl.when((o >= z) & has_l)
        def _():
            z_full(q, o, 1).wait_send()
            z_part(q, o, 1).wait_send()

        y_first(q, o, y).wait_send()
        return 0

    lax.fori_loop(0, Q * nz, drain, 0)
    for q in range(Q):
        y_last(q, y).wait_send()
    for p in range(pairs):
        for h in range(2):
            to_sibling(2 * p + 1 - c, p, h).wait_send()
        to_opposite(2 * p + c, p).wait_send()


def fused(nb, integrals, block_mask, amplitudes, pair_batches):
    rows_out, number = integrals.shape
    R, occ = amplitudes.shape
    Q, nz = NB // 2, nb // 2
    beta = max(16, R // 6 // 16 * 16)
    dma = pltpu.SemaphoreType.DMA
    return pl.pallas_call(
        functools.partial(kernel, nz, beta),
        out_shape=jax.ShapeDtypeStruct((occ // 4, rows_out), jnp.bfloat16),
        in_specs=[
            pl.BlockSpec(memory_space=pltpu.SMEM),
            pl.BlockSpec(memory_space=pltpu.SMEM),
            pl.BlockSpec(memory_space=pltpu.VMEM),
            pl.BlockSpec(memory_space=pl.ANY),
        ],
        out_specs=pl.BlockSpec(memory_space=pltpu.VMEM),
        scratch_shapes=[
            pltpu.VMEM((Q, nb, R, 2 * BATCH), jnp.bfloat16),
            pltpu.VMEM((rows_out, number), jnp.bfloat16),
            pltpu.VMEM((Q, 2, rows_out, BATCH), jnp.float32),
            pltpu.VMEM((Q // 2, 2, rows_out, BATCH), jnp.float32),
            pltpu.VMEM((Q // 2, rows_out, BATCH), jnp.float32),
            dma,
            dma((Q, 2, nz)), dma((Q, 2, nz)), dma((Q, nz)), dma((Q, nz)),
            dma((Q, nz)), dma((Q, nz)), dma((Q,)), dma((Q,)),
            dma((Q // 2, 2)), dma((Q // 2, 2)), dma((Q // 2,)), dma((Q // 2,)),
        ],
        compiler_params=pltpu.CompilerParams(
            collective_id=0, has_side_effects=True, vmem_limit_bytes=56 * 2**20
        ),
        cost_estimate=pl.CostEstimate(
            flops=2 * occ * rows_out * number,
            bytes_accessed=2 * rows_out * number + 2 * nb * R * occ,
            transcendentals=0,
        ),
    )(block_mask, pair_batches, amplitudes, integrals)


def solution(mesh):
    ng, nb = mesh.shape["grp"], mesh.shape["blk"]
    takes = ng == 4 and nb % 2 == 0 and nb // 2 >= LAG + 2
    in_specs = (P("blk", "grp"), P("blk", "grp"), P(("grp", "blk"), None), P())
    return jax.shard_map(
        functools.partial(fused, nb) if takes else plain,
        mesh=mesh, in_specs=in_specs, out_specs=P("grp", "blk"), check_vma=False,
    )
```

```python
import functools

import jax
import jax.numpy as jnp
from jax import lax
from jax.experimental import pallas as pl
from jax.experimental.pallas import tpu as pltpu
from jax.sharding import PartitionSpec as P

BLOCK = 128
BATCH = 128
NB = 8
LAG = 2
MESH = pl.DeviceIdType.MESH


def plain(integrals, block_mask, amplitudes, pair_batches):
    rows_in = amplitudes.shape[0]
    grouped = amplitudes.reshape(rows_in, NB, BATCH)
    chosen = jnp.take(grouped, pair_batches, axis=1).reshape(rows_in, NB * BATCH)
    out_rows = integrals.shape[0]
    fragment = lax.all_gather(chosen, "blk", axis=0, tiled=True)
    number = fragment.shape[0]
    mcols = block_mask.astype(jnp.bfloat16)
    tiled = (
        integrals.reshape(out_rows // BLOCK, BLOCK, number // BLOCK, BLOCK)
        * mcols[:, None, :, None]
    )
    masked = tiled.reshape(out_rows, number)
    partial_sum = lax.dot_general(
        fragment, masked, (((0,), (1,)), ((), ())), preferred_element_type=jnp.float32
    )
    owned = lax.psum_scatter(partial_sum, "grp", scatter_dimension=0, tiled=True)
    return owned.astype(jnp.bfloat16)


def kernel(
    nz, beta,
    mask_ref, order_ref, amp_ref, int_ref, out_ref,
    T, V, acc, sib, far,
    v_sem, zfs, zbs, zfr, zbr, yas, yar, ybs, ybr, sibs, sibr, fars, farr,
):
    g, b = lax.axis_index("grp"), lax.axis_index("blk")
    x, c = g // 2, g % 2
    z, y = b // 2, b % 2
    Q, nb, R, _ = T.shape
    pairs = Q // 2
    rows_out = V.shape[0]
    alpha = R - beta
    has_l, has_r = z > 0, z < nz - 1
    sibling = (x * 2 + 1 - c, b)
    opposite = ((1 - x) * 2 + c, b)
    partner = (g, z * 2 + 1 - y)
    toward = ((g, jnp.minimum(z + 1, nz - 1) * 2 + y), (g, jnp.maximum(z - 1, 0) * 2 + y))

    def remote(src, dst, send, recv, device):
        return pltpu.make_async_remote_copy(
            src_ref=src, dst_ref=dst, send_sem=send, recv_sem=recv,
            device_id=device, device_id_type=MESH,
        )

    def z_full(q, o, d):
        ref = T.at[q, 2 * o + y]
        return remote(ref, ref, zfs.at[q, d, o], zfr.at[q, o], toward[d])

    def z_part(q, o, d):
        ref = T.at[q, 2 * o + 1 - y, pl.ds(alpha, beta)]
        return remote(ref, ref, zbs.at[q, d, o], zbr.at[q, o], toward[d])

    def y_first(q, o, v):
        ref = T.at[q, 2 * o + v, pl.ds(0, alpha)]
        return remote(ref, ref, yas.at[q, o], yar.at[q, o], partner)

    def y_last(q, v):
        ref = T.at[q, 2 * z + v, pl.ds(alpha, beta)]
        return remote(ref, ref, ybs.at[q], ybr.at[q], partner)

    def to_sibling(q, j, h):
        return remote(acc.at[q, h], sib.at[j, h], sibs.at[j, h], sibr.at[j, h], sibling)

    def to_opposite(q, j):
        return remote(acc.at[q, 1 - x], far.at[j], fars.at[j], farr.at[j], opposite)

    load_v = pltpu.make_async_copy(int_ref, V, v_sem)
    load_v.start()

    barrier = pltpu.get_barrier_semaphore()
    for device in (sibling, opposite, partner):
        pl.semaphore_signal(barrier, inc=1, device_id=device, device_id_type=MESH)
    for d, there in ((0, has_r), (1, has_l)):
        @pl.when(there)
        def _():
            pl.semaphore_signal(barrier, inc=1, device_id=toward[d], device_id_type=MESH)

    def choose(q):
        for half in range(2):
            k = (NB // 2) * half + (NB // 4) * (q % 2) + q // 2
            picks = [
                jnp.full((16, BATCH), jnp.where(order_ref[k] == n, 1.0, 0.0)).astype(jnp.bfloat16)
                for n in range(NB)
            ]

            def some(i, _):
                rows = pl.ds(pl.multiple_of(i * 128, 128), 128)
                total = None
                for n in range(NB):
                    batch = amp_ref[rows, n * BATCH:(n + 1) * BATCH]
                    term = batch * jnp.tile(picks[n], (8, 1))
                    total = term if total is None else total + term
                T[q, b, rows, half * BATCH:(half + 1) * BATCH] = total
                return 0

            lax.fori_loop(0, R // 128, some, 0)

    choose(0)
    choose(1)
    pl.semaphore_wait(barrier, 3 + has_r.astype(jnp.int32) + has_l.astype(jnp.int32))

    def gemm(q, shard):
        tile = min(256, rows_out)

        @pl.when(q == 0)
        def _():
            mask_tiles(shard)

        def rows_of(i, _):
            rows = pl.ds(pl.multiple_of(i * tile, tile), tile)
            cols = pl.ds(pl.multiple_of(shard * R, 128), R)
            res = jnp.dot(V[rows, cols], T[q, shard], preferred_element_type=jnp.float32)
            acc[q, 0, rows, :] += res[:, :BATCH]
            acc[q, 1, rows, :] += res[:, BATCH:]
            return 0

        lax.fori_loop(0, rows_out // tile, rows_of, 0)

    def start_own(p):
        for qi in range(2):
            q = 2 * p + qi
            y_last(q, y).start()
            for d, there in ((0, has_r), (1, has_l)):
                @pl.when(there)
                def _():
                    z_full(q, z, d).start()
            y_first(q, z, y).start()
        for qi in range(2):
            q = 2 * p + qi
            y_last(q, 1 - y).wait_recv()
            for d, there in ((0, has_r), (1, has_l)):
                @pl.when(there)
                def _():
                    z_part(q, z, d).start()

    def forward(p, s):
        for qi in range(2):
            q = 2 * p + qi
            for d, there in ((0, has_r), (1, has_l)):
                o = z - s if d == 0 else z + s

                @pl.when((o >= 0) & (o < nz))
                def _():
                    z_full(q, o, d).wait_recv()

                    @pl.when(there)
                    def _():
                        z_full(q, o, d).start()

                    y_first(q, o, y).start()
                    z_part(q, o, d).wait_recv()

                    @pl.when(there)
                    def _():
                        z_part(q, o, d).start()

    def each(p, s, act, low=0, high=4):
        def one(i, _):
            q, d = 2 * p + i // 2, i % 2
            o = z + s * (2 * d - 1)

            @pl.when((o >= 0) & (o < nz) & ((d == 0) | (s > 0)))
            def _():
                act(q, o)
            return 0

        lax.fori_loop(low, high, one, 0)

    def lagged(q, o):
        y_first(q, o, 1 - y).wait_recv()
        gemm(q, 2 * o + 1 - y)

    def hand_over(p, qi):
        @pl.when(c != qi)
        def _():
            to_sibling(2 * p + qi, p, 1 - x).start()
            to_sibling(2 * p + qi, p, x).start()

    def reduce_a(p):
        for qi in range(2):
            hand_over(p, qi)

    def reduce_b(p):
        q = 2 * p + c
        to_sibling(q, p, 1 - x).wait_recv()
        acc[q, 1 - x] += sib[p, 1 - x]
        to_opposite(q, p).start()
        to_sibling(q, p, x).wait_recv()
        acc[q, x] += sib[p, x]

    def reduce_c(p):
        q = 2 * p + c
        to_opposite(q, p).wait_recv()

        def cols(i, _):
            rows = pl.ds(pl.multiple_of(i * BLOCK, BLOCK), BLOCK)
            total = acc[q, x, rows, :] + far[p, rows, :]
            out_ref[pl.ds(pl.multiple_of(p * BATCH, BATCH), BATCH), rows] = total.T.astype(jnp.bfloat16)
            return 0

        lax.fori_loop(0, rows_out // BLOCK, cols, 0)

    def mask_tiles(shard):
        def tile(i, _):
            r, k = i // (R // BLOCK), shard * (R // BLOCK) + i % (R // BLOCK)
            at = (
                pl.ds(pl.multiple_of(r * BLOCK, BLOCK), BLOCK),
                pl.ds(pl.multiple_of(k * BLOCK, BLOCK), BLOCK),
            )
            keep = jnp.full((BLOCK, BLOCK), mask_ref[r, k].astype(jnp.float32)).astype(jnp.bfloat16)
            V[at] = V[at] * keep
            return 0

        lax.fori_loop(0, (rows_out // BLOCK) * (R // BLOCK), tile, 0)

    def step(t, _):
        p, s = t // nz, t % nz

        @pl.when(t < pairs * nz)
        def _():
            @pl.when(s == 0)
            def _():
                start_own(p)

            @pl.when(s > 0)
            def _():
                forward(p, s)

            @pl.when(t == 0)
            def _():
                for q in range(2, Q):
                    choose(q)
                acc[...] = jnp.zeros_like(acc)
                load_v.wait()

            each(p, s, lambda q, o: gemm(q, 2 * o + y))

        @pl.when(t >= LAG)
        def _():
            late = jnp.maximum(t - LAG, 0)
            each(late // nz, late % nz, lagged)

        done = p - 1
        for at, act in ((LAG - 1, reduce_a), (LAG, reduce_b), (LAG + 1, reduce_c)):
            @pl.when((done >= 0) & (done < pairs - 1) & (s == at))
            def _():
                act(done)
        return 0

    lax.fori_loop(0, pairs * nz + LAG - 1, step, 0)
    last = pairs - 1
    for qi in range(2):
        each(last, nz - 1, lagged, 2 * qi, 2 * qi + 2)
        hand_over(last, qi)

        @pl.when(c == qi)
        def _():
            reduce_b(last)

    reduce_c(last)

    def drain(i, _):
        q, o = i // nz, i % nz

        @pl.when((o <= z) & has_r)
        def _():
            z_full(q, o, 0).wait_send()
            z_part(q, o, 0).wait_send()

        @pl.when((o >= z) & has_l)
        def _():
            z_full(q, o, 1).wait_send()
            z_part(q, o, 1).wait_send()

        y_first(q, o, y).wait_send()
        return 0

    lax.fori_loop(0, Q * nz, drain, 0)
    for q in range(Q):
        y_last(q, y).wait_send()
    for p in range(pairs):
        for h in range(2):
            to_sibling(2 * p + 1 - c, p, h).wait_send()
        to_opposite(2 * p + c, p).wait_send()


def fused(nb, integrals, block_mask, amplitudes, pair_batches):
    rows_out, number = integrals.shape
    R, occ = amplitudes.shape
    Q, nz = NB // 2, nb // 2
    beta = max(32, R // 10 // 32 * 32)
    dma = pltpu.SemaphoreType.DMA
    return pl.pallas_call(
        functools.partial(kernel, nz, beta),
        out_shape=jax.ShapeDtypeStruct((occ // 4, rows_out), jnp.bfloat16),
        in_specs=[
            pl.BlockSpec(memory_space=pltpu.SMEM),
            pl.BlockSpec(memory_space=pltpu.SMEM),
            pl.BlockSpec(memory_space=pltpu.VMEM),
            pl.BlockSpec(memory_space=pl.ANY),
        ],
        out_specs=pl.BlockSpec(memory_space=pltpu.VMEM),
        scratch_shapes=[
            pltpu.VMEM((Q, nb, R, 2 * BATCH), jnp.bfloat16),
            pltpu.VMEM((rows_out, number), jnp.bfloat16),
            pltpu.VMEM((Q, 2, rows_out, BATCH), jnp.float32),
            pltpu.VMEM((Q // 2, 2, rows_out, BATCH), jnp.float32),
            pltpu.VMEM((Q // 2, rows_out, BATCH), jnp.float32),
            dma,
            dma((Q, 2, nz)), dma((Q, 2, nz)), dma((Q, nz)), dma((Q, nz)),
            dma((Q, nz)), dma((Q, nz)), dma((Q,)), dma((Q,)),
            dma((Q // 2, 2)), dma((Q // 2, 2)), dma((Q // 2,)), dma((Q // 2,)),
        ],
        compiler_params=pltpu.CompilerParams(
            collective_id=0, has_side_effects=True, vmem_limit_bytes=56 * 2**20
        ),
        cost_estimate=pl.CostEstimate(
            flops=2 * occ * rows_out * number,
            bytes_accessed=2 * rows_out * number + 2 * nb * R * occ,
            transcendentals=0,
        ),
    )(block_mask, pair_batches, amplitudes, integrals)


def solution(mesh):
    ng, nb = mesh.shape["grp"], mesh.shape["blk"]
    takes = ng == 4 and nb % 2 == 0 and nb // 2 >= LAG + 2
    in_specs = (P("blk", "grp"), P("blk", "grp"), P(("grp", "blk"), None), P())
    return jax.shard_map(
        functools.partial(fused, nb) if takes else plain,
        mesh=mesh, in_specs=in_specs, out_specs=P("grp", "blk"), check_vma=False,
    )
```
